512 devices in a mesh: branch: 16 (over y, core), leaf: 32 (over z, x).
Axes of the slice: x: 4, y: 8, z: 8, core: 2. Of those that a mesh axis runs over, the one named last changes fastest.
Arguments:
- vectors: bfloat16 [32, 786432], P(None, ('branch', 'leaf')), may hold values from -6 to 6
- leaf_cluster_bases: bfloat16 [3072, 256, 128], P(('branch', 'leaf')), may hold values from -0.375 to 0.375
- transfers: bfloat16 [3072, 128, 128], P(('branch', 'leaf')), may hold values from -0.5 to 0.5
- parents: int32 [3072], P(('branch', 'leaf')), may hold values from 0 to 1023, as said below
- leaf_pairs: int32 [16384, 2], P(('branch', 'leaf')), may hold values from 0 to 3071, as said below
- live_pairs: int32 [512], P(('branch', 'leaf')), may hold values from 8 to 32
- couplings: bfloat16 [16384, 128, 128], P(('branch', 'leaf')), may hold values from -0.25 to 0.25
- upper_pairs: int32 [2048, 2], P(('branch', 'leaf')), may hold values from 0 to 1023, as said below
- upper_coupling_matrices: bfloat16 [2048, 128, 128], P(('branch', 'leaf')), may hold values from -0.1875 to 0.1875
- self_blocks: bfloat16 [3072, 256, 256], P(('branch', 'leaf')), may hold values from -0.375 to 0.375
- near_pairs: int32 [4096, 2], P(('branch', 'leaf')), may hold values from 0 to 3071, as said below
- near_blocks: bfloat16 [4096, 256, 256], P(('branch', 'leaf')), may hold values from -0.25 to 0.25
Outputs:
- product: bfloat16 [32, 786432], P(None, ('branch', 'leaf'))
The draws below stay inside these ranges and needn't reach their ends.
Inputs may be any that keep to these rules, and one draw needn't show every extreme that they name: parents[c] // 2 == c // 6: a leaf's parent lies on the leaf's device. `leaf_pairs`: slot k is held by device k // 32 (devices counted branch first). Its first cluster lies on that device, its second on another device of the same branch; at most 2 of one device's slots have their second cluster on one given device. `upper_pairs`: upper pair k is held by device k // 4; its first cluster lies on that device, its second on a device of another branch with the same leaf index. `near_pairs`: near pair k is held by device k // 8; both its clusters lie on that device and differ.
All inputs are finite; a program needn't handle non-finite values.
Results may differ from the reference program's by a relative error of at most 0.0052.
Values may be sent and summed in bfloat16 or wider, within the bound.
A program may use at most 64 MiB of HBM per device.

```python
import jax
import jax.numpy as jnp
from jax import lax

NV = 32
K = 128
LEAF = 256
CPD = 6
P1D = 2
PAIRS_DEV = 32
PAIRS1_DEV = 4
NEAR_DEV = 8
MOST = 2
C0 = 3072
POINTS = 786432
PAIRS = 16384
UPPER = 2048
NEARS = 4096
N_BRANCH = 16
N_LEAF = 32


def draw_parents(key, part):
    key = jax.random.fold_in(key, 11)
    device_count = N_BRANCH * N_LEAF
    local_parent = jax.random.randint(key, (device_count, CPD), 0, P1D)
    owners = jnp.arange(device_count, dtype=jnp.int32)[:, None] * P1D
    return (owners + local_parent).reshape(-1).astype(jnp.int32)


def draw_live_pairs(key, part):
    key = jax.random.fold_in(key, 12)
    device_count = N_BRANCH * N_LEAF
    key_counts, key_top = jax.random.split(key)
    drawn_counts = jax.random.randint(key_counts, (device_count,), PAIRS_DEV // 4, PAIRS_DEV + 1)
    busiest = jax.random.randint(key_top, (), 0, device_count)
    device_ids = jnp.arange(device_count, dtype=jnp.int32)
    return jnp.where(device_ids == busiest, PAIRS_DEV, drawn_counts).astype(jnp.int32)


def draw_leaf_pairs(key, part):
    key = jax.random.fold_in(key, 13)
    device_count = N_BRANCH * N_LEAF
    key_score, key_hot, key_far, key_own = jax.random.split(key, 4)
    slot_total = (N_LEAF - 1) * MOST
    slot_ids = jnp.arange(slot_total, dtype=jnp.int32)
    scores = jax.random.randint(key_score, (device_count, slot_total), 0, 2 ** 20) * slot_total + slot_ids[None, :]
    hot_leaf = jax.random.randint(key_hot, (N_BRANCH,), 0, N_LEAF)
    device_ids = jnp.arange(device_count, dtype=jnp.int32)
    branch_ids = device_ids // N_LEAF
    leaf_ids = device_ids % N_LEAF
    hot_offset = (hot_leaf[branch_ids] - leaf_ids) % N_LEAF
    offsets = slot_ids // MOST + 1
    forced = offsets[None, :] == hot_offset[:, None]
    keyed = jnp.where(forced, scores - 2 ** 21 * slot_total, scores)
    chosen = jnp.argsort(keyed, axis=1)[:, :PAIRS_DEV].astype(jnp.int32)
    peers = (leaf_ids[:, None] + chosen // MOST + 1) % N_LEAF
    far_local = jax.random.randint(key_far, (device_count, PAIRS_DEV), 0, CPD)
    own_local = jax.random.randint(key_own, (device_count, PAIRS_DEV), 0, CPD)
    second = (branch_ids[:, None] * N_LEAF + peers) * CPD + far_local
    first_side = device_ids[:, None] * CPD + own_local
    return jnp.stack([first_side, second], axis=-1).reshape(device_count * PAIRS_DEV, 2).astype(jnp.int32)


def draw_upper_pairs(key, part):
    key = jax.random.fold_in(key, 14)
    device_count = N_BRANCH * N_LEAF
    key_own, key_branch, key_far = jax.random.split(key, 3)
    device_ids = jnp.arange(device_count, dtype=jnp.int32)[:, None]
    pair_shape = (device_count, PAIRS1_DEV)
    own_parent = jax.random.randint(key_own, pair_shape, 0, P1D)
    branch_step = jax.random.randint(key_branch, pair_shape, 1, N_BRANCH)
    far_parent = jax.random.randint(key_far, pair_shape, 0, P1D)
    far_branch = (device_ids // N_LEAF + branch_step) % N_BRANCH
    far_device = far_branch * N_LEAF + device_ids % N_LEAF
    first_side = device_ids * P1D + own_parent
    second = far_device * P1D + far_parent
    return jnp.stack([first_side, second], axis=-1).reshape(device_count * PAIRS1_DEV, 2).astype(jnp.int32)


def draw_near_pairs(key, part):
    key = jax.random.fold_in(key, 15)
    device_count = N_BRANCH * N_LEAF
    key_own, key_step = jax.random.split(key)
    device_ids = jnp.arange(device_count, dtype=jnp.int32)[:, None]
    pair_shape = (device_count, NEAR_DEV)
    own_local = jax.random.randint(key_own, pair_shape, 0, CPD)
    step_local = jax.random.randint(key_step, pair_shape, 1, CPD)
    first_side = device_ids * CPD + own_local
    second = device_ids * CPD + (own_local + step_local) % CPD
    return jnp.stack([first_side, second], axis=-1).reshape(device_count * NEAR_DEV, 2).astype(jnp.int32)


def block_levels(stream_key, dims, shards, least, top_value):
    gain, own = 1.0, jax.random.fold_in(stream_key, 6)
    for position, shards_of in shards:
        steps = jnp.exp(jax.random.uniform(jax.random.fold_in(own, position), (shards_of,), jnp.float32, least / len(shards), top_value / len(shards)))
        gain = gain * jnp.repeat(steps, dims[position] // shards_of).reshape([-1 if axis == position else 1 for axis in range(len(dims))])
    return gain


def normal_values(own_key, extent, deviation, reach, pieces=(), kind=jnp.bfloat16):
    array = deviation * jax.random.normal(own_key, extent, jnp.float32)
    if pieces:
        array = array * block_levels(own_key, extent, pieces, -0.22, 0.18)
    return jnp.clip(array, -reach, reach).astype(kind)


def setup_inputs(seed: int = 0) -> dict:
    keys = jax.random.split(jax.random.key(seed), 13)
    vectors = normal_values(keys[0], (NV, POINTS), 1.0, 6.0, ((1, 512),))
    leaf_cluster_bases = normal_values(keys[1], (C0, LEAF, K), LEAF ** -0.5, 0.375, ((0, 512),))
    transfers = normal_values(keys[2], (C0, K, K), K ** -0.5, 0.5, ((0, 512),))
    parents = draw_parents(jax.random.fold_in(keys[12], 71), 0)
    leaf_pairs = draw_leaf_pairs(jax.random.fold_in(keys[12], 71), 0)
    live_pairs = draw_live_pairs(jax.random.fold_in(keys[12], 71), 0)
    couplings = normal_values(keys[6], (PAIRS, K, K), (4 * K) ** -0.5, 0.25, ((0, 512),))
    upper_pairs = draw_upper_pairs(jax.random.fold_in(keys[12], 71), 0)
    upper_coupling_matrices = normal_values(keys[8], (UPPER, K, K), (8 * K) ** -0.5, 0.1875, ((0, 512),))
    self_blocks = normal_values(keys[9], (C0, LEAF, LEAF), LEAF ** -0.5, 0.375, ((0, 512),))
    near_pairs = draw_near_pairs(jax.random.fold_in(keys[12], 71), 0)
    near_blocks = normal_values(keys[11], (NEARS, LEAF, LEAF), (2 * LEAF) ** -0.5, 0.25, ((0, 512),))
    return dict(vectors=vectors, leaf_cluster_bases=leaf_cluster_bases, transfers=transfers, parents=parents, leaf_pairs=leaf_pairs, live_pairs=live_pairs, couplings=couplings, upper_pairs=upper_pairs, upper_coupling_matrices=upper_coupling_matrices, self_blocks=self_blocks, near_pairs=near_pairs, near_blocks=near_blocks)


def pair_terms(coeffs, pairs, matrices, weight, group_count):
    pair_blocks = pairs.reshape(group_count, -1, 2)
    matrix_blocks = matrices.reshape((group_count, -1) + matrices.shape[1:])
    weight_blocks = weight.reshape(group_count, -1)

    def per_device(device_block):
        chosen, matrix_part, weight_part = device_block
        first_side = coeffs[chosen[:, 0]].astype(jnp.float32)
        second = coeffs[chosen[:, 1]].astype(jnp.float32)
        matrix_float = matrix_part.astype(jnp.float32)
        to_first = jnp.einsum("nvk,nkj->nvj", second, matrix_float) * weight_part[:, None, None]
        to_second = jnp.einsum("nvj,nkj->nvk", first_side, matrix_float) * weight_part[:, None, None]
        return to_first, to_second

    to_first, to_second = lax.map(per_device, (pair_blocks, matrix_blocks, weight_blocks))
    to_first = to_first.reshape((-1,) + to_first.shape[2:])
    to_second = to_second.reshape((-1,) + to_second.shape[2:])
    field = jnp.zeros(coeffs.shape, jnp.float32)
    field = field.at[pairs[:, 0]].add(to_first)
    return field.at[pairs[:, 1]].add(to_second)


def reference(vectors, leaf_cluster_bases, transfers, parents, leaf_pairs, live_pairs, couplings, upper_pairs, upper_coupling_matrices, self_blocks, near_pairs, near_blocks):
    device_count = N_BRANCH * N_LEAF
    cluster_total = leaf_cluster_bases.shape[0]
    vector_columns = jnp.transpose(vectors.reshape(NV, cluster_total, LEAF), (1, 0, 2))
    leaf_coefficients = jnp.einsum("jba,jar->jbr", vector_columns.astype(jnp.float32), leaf_cluster_bases.astype(jnp.float32)).astype(jnp.bfloat16)
    lifted = jnp.einsum("cvk,ckj->cvj", leaf_coefficients.astype(jnp.float32), transfers.astype(jnp.float32))
    parent_coeffs = jnp.zeros((P1D * device_count, NV, K), jnp.float32).at[parents].add(lifted).astype(jnp.bfloat16)
    slot_index = jnp.arange(leaf_pairs.shape[0], dtype=jnp.int32)
    live_weight = ((slot_index % PAIRS_DEV) < live_pairs[slot_index // PAIRS_DEV]).astype(jnp.float32)
    leaf_field = pair_terms(leaf_coefficients, leaf_pairs, couplings, live_weight, device_count)
    upper_weight = jnp.ones((upper_pairs.shape[0],), jnp.float32)
    parent_field = pair_terms(parent_coeffs, upper_pairs, upper_coupling_matrices, upper_weight, device_count).astype(jnp.bfloat16)
    lowered = jnp.einsum("cvj,ckj->cvk", parent_field[parents].astype(jnp.float32), transfers.astype(jnp.float32))
    total_leaf_count = (leaf_field + lowered).astype(jnp.bfloat16)
    near_weight = jnp.ones((near_pairs.shape[0],), jnp.float32)
    nearby_field_blocks = pair_terms(vector_columns, near_pairs, near_blocks, near_weight, device_count)
    nearby_field_blocks = nearby_field_blocks + jnp.einsum("cvl,clm->cvm", vector_columns.astype(jnp.float32), self_blocks.astype(jnp.float32))
    product_output = nearby_field_blocks + jnp.einsum("gbj,gxj->gbx", total_leaf_count.astype(jnp.float32), leaf_cluster_bases.astype(jnp.float32))
    return jnp.transpose(product_output, (1, 0, 2)).reshape(NV, cluster_total * LEAF).astype(jnp.bfloat16)
```

```python
import jax
import jax.numpy as jnp
from jax import lax
from jax.experimental import pallas as pl
from jax.experimental.pallas import tpu as pltpu
from jax.sharding import PartitionSpec as P

CPD = 6
P1D = 2
CORES = 2
XDIM = 4
MOST = 2
LANES = 128
FAR = 1000
MESH = pl.DeviceIdType.MESH
F32 = jnp.float32
BF16 = jnp.bfloat16
UNROLL = 8


def dot_nn(a, b):
    return jnp.dot(a, b, preferred_element_type=F32)


def dot_nt(a, b):
    return lax.dot_general(a, b, (((1,), (1,)), ((), ())), preferred_element_type=F32)


def make_kernel(yd, zd):
    cd, xd = CORES, XDIM
    per_x = zd * MOST
    half = zd // 2

    def zi_of(dz):
        dz %= zd
        if dz == 0:
            return 0
        return 2 * dz - 1 if dz <= half else 2 * (zd - dz)

    dz_of = [0] * zd
    for d in range(zd):
        dz_of[zi_of(d)] = d
    groups = [[0]] + [[2 * h - 1, 2 * h] for h in range(1, half)] + [[zd - 1]]
    column = [(dy, dc) for dc in range(cd) for dy in range(yd) if dy or dc]

    def kernel(
        vec_h, bas_h, tra_h, par_s, lp_v, live_s, cou_h, up_s, uco_h, sel_h, np_s, nea_h,
        out_ref,
        vec, bas, tra, cou, uco, sel, nea,
        tab, tabs, p_own, s_a, r_a, s_d, r_d, t_buf, zsend, zrecv, d_own,
        pbuf, u_send, u_recv, pf,
        x3, nacc, lacc,
        lsem, ssem, rsem, *zbuf,
    ):
        b = lax.axis_index("branch")
        l = lax.axis_index("leaf")
        y, c, z, x = b // cd, b % cd, l // xd, l % xd
        pair_count = cou_h.shape[0]
        upper_count = uco_h.shape[0]
        near_count = nea_h.shape[0]
        width = x3.shape[2]

        def at(dy=0, dc=0, dz=0, dx=0):
            yy, cc = (y + dy) % yd, (c + dc) % cd
            zz, xx = (z + dz) % zd, (x + dx) % xd
            return (yy * cd + cc, zz * xd + xx)

        loads = {}
        for i, (name, src, dst) in enumerate(
            (("vec", vec_h, vec), ("bas", bas_h, bas), ("tra", tra_h, tra), ("cou", cou_h, cou),
             ("uco", uco_h, uco), ("sel", sel_h, sel), ("nea", nea_h, nea))
        ):
            loads[name] = pltpu.make_async_copy(src, dst, lsem.at[i])
            loads[name].start()

        barrier = pltpu.get_barrier_semaphore()
        partners = [at(dz=d) for d in range(1, zd)] + [at(dx=d) for d in range(1, xd)]
        partners += [at(dy=dy, dc=dc) for dy, dc in column]
        for device in partners:
            pl.semaphore_signal(barrier, inc=1, device_id=device, device_id_type=MESH)

        count = [0]
        sent = []

        def send(src, dst, device):
            i = count[0]
            count[0] += 1
            copy = pltpu.make_async_remote_copy(
                src_ref=src, dst_ref=dst, send_sem=ssem.at[i], recv_sem=rsem.at[i],
                device_id=device, device_id_type=MESH,
            )
            copy.start()
            sent.append(copy)
            return copy

        def add_where(acc, terms, i):
            for where, term in terms:
                acc = acc + jnp.where(where == i, term, 0.0)
            return acc

        live = live_s[0]
        first = lp_v[0:1, :] % CPD
        second = lp_v[1:2, :] % (zd * xd * CPD)
        owner = (second * 10923) >> 16
        second_c = second - owner * CPD
        oz, ox = owner // xd, owner % xd
        odz = (oz - z + zd) % zd
        odx = (ox - x + xd) % xd
        ozi = jnp.where(odz <= half, 2 * odz - 1, 2 * (zd - odz))
        ozi = jnp.where(odz == 0, 0, ozi)
        peer = odx * zd + ozi
        sub = lax.broadcasted_iota(jnp.int32, (pair_count, pair_count), 0)
        lane = lax.broadcasted_iota(jnp.int32, (pair_count, pair_count), 1)
        eye = sub == lane

        def to_col(row):
            return jnp.sum(jnp.where(eye, row, 0), axis=1, keepdims=True)

        peer_col = to_col(peer)
        rank_col = jnp.sum(
            jnp.where((peer == peer_col) & (lane < sub), 1, 0), axis=1, keepdims=True
        )
        sub_col = lax.broadcasted_iota(jnp.int32, (pair_count, 1), 0)
        pos_col = jnp.where(sub_col < live, peer_col * MOST + rank_col, FAR)
        slot_lane = lax.broadcasted_iota(jnp.int32, (pair_count, LANES), 1)
        hit = pos_col == slot_lane

        def by_slot(col, none):
            return none - jnp.sum(jnp.where(hit, none - col, 0), axis=0, keepdims=True)

        pair_of = by_slot(sub_col, pair_count)
        tab[0] = jnp.zeros_like(tab[0])
        tab[0, 0:1, :] = pair_of
        tab[0, 1:2, :] = by_slot(to_col(second_c), 0)
        tab[0, 2:3, :] = by_slot(to_col(first), CPD)
        tab[0, 3:4, :] = jnp.minimum(pair_of, pair_count - 1)
        tab[0, 4:5, 0:pair_count] = first
        own_tab = pltpu.make_async_copy(tab.at[0], tabs.at[0], lsem.at[7])
        own_tab.start()

        loads["vec"].wait()
        loads["bas"].wait()
        for i in range(CPD):
            xi = vec[:, i * width:(i + 1) * width]
            x3[i] = xi
            zbuf[0][i] = dot_nn(xi, bas[i]).astype(BF16)

        loads["tra"].wait()
        lifted = [(par_s[i] % P1D, dot_nn(zbuf[0][i], tra[i])) for i in range(CPD)]
        for p in range(P1D):
            acc = add_where(jnp.zeros(lifted[0][1].shape, F32), lifted, p).astype(BF16)
            p_own[p] = acc
            pbuf[0, 0, p] = acc

        loads["cou"].wait()
        own_tab.wait()
        t_buf[pair_count] = jnp.zeros_like(t_buf[pair_count])

        def second_body(i, carry):
            for u in range(UNROLL):
                k = i * UNROLL + u
                f = tabs[0, 4, k]
                t_buf[k] = dot_nt(zbuf[0][f], cou[k]).astype(BF16)
            return carry

        lax.fori_loop(0, pair_count // UNROLL, second_body, 0)
        for dx in range(xd):
            buf = r_d if dx == 0 else s_d
            for s in range(dx * per_x, (dx + 1) * per_x):
                buf[s] = t_buf[tabs[0, 0, s]]

        loads["uco"].wait()
        u_first = [up_s[0, k] % P1D for k in range(upper_count)]
        u_row, u_dy, u_dc = [], [], []
        for k in range(upper_count):
            q = up_s[1, k]
            far_b = q // (P1D * zd * xd)
            u_row.append(q % P1D)
            u_dy.append((far_b // cd - y + yd) % yd)
            u_dc.append((far_b % cd - c + cd) % cd)
        u_terms = [
            ((u_dc[k] * yd + u_dy[k]) * P1D + u_row[k], dot_nt(p_own[u_first[k]], uco[k]))
            for k in range(upper_count)
        ]
        for dy, dc in column:
            for p in range(P1D):
                acc = jnp.zeros(u_terms[0][1].shape, F32)
                u_send[dc, dy, p] = add_where(acc, u_terms, (dc * yd + dy) * P1D + p).astype(BF16)

        pl.semaphore_wait(barrier, len(partners))

        def ring(h):
            if h < half:
                src_l, dst_l = zbuf[zi_of(h - 1)], zbuf[zi_of(h)]
                src_r, dst_r = zbuf[zi_of(1 - h)], zbuf[zi_of(-h)]
            else:
                cut = CPD // 2
                src_l, dst_l = zbuf[zi_of(h - 1)].at[0:cut], zbuf[zi_of(h)].at[0:cut]
                src_r, dst_r = zbuf[zi_of(1 - h)].at[cut:CPD], zbuf[zi_of(-h)].at[cut:CPD]
            return [send(src_l, dst_l, at(dz=-1)), send(src_r, dst_r, at(dz=1))]

        def send_slots(src, dst, gi):
            lo, n = groups[gi][0] * MOST, len(groups[gi]) * MOST
            return [
                send(
                    src.at[pl.ds(dx * per_x + lo, n)],
                    dst.at[pl.ds(((-dx) % xd) * per_x + lo, n)],
                    at(dx=dx),
                )
                for dx in range(1, xd)
            ]

        tab_copies = [send(tab.at[0], tab.at[(-d) % xd], at(dx=d)) for d in range(1, xd)]
        hop = ring(1)
        d_copies = {gi: send_slots(s_d, r_d, gi) for gi in reversed(range(len(groups)))}
        b_copies, c_copies = [], []
        for dy, dc in column:
            there = ((-dc) % cd, (-dy) % yd)
            b_copies.append(send(p_own, pbuf.at[there[0], there[1]], at(dy=dy, dc=dc)))
            c_copies.append(
                send(u_send.at[dc, dy], u_recv.at[there[0], there[1]], at(dy=dy, dc=dc))
            )

        for copy in tab_copies:
            copy.wait_recv()
        peer_tab = pltpu.make_async_copy(tab.at[1:xd], tabs.at[1:xd], lsem.at[8])
        peer_tab.start()
        peer_tab.wait()

        def answer(gi):
            for dx in range(xd):
                for zi in groups[gi]:
                    for j in range(MOST):
                        r = tabs[dx, 1, ((-dx) % xd) * per_x + zi * MOST + j]
                        buf = r_a if dx == 0 else s_a
                        buf[dx * per_x + zi * MOST + j] = zbuf[zi][r]
            return send_slots(s_a, r_a, gi)

        def near_pairs(lo, hi):
            terms = []
            for k in range(lo, hi):
                f, s = np_s[0, k] % CPD, np_s[1, k] % CPD
                terms.append((f, dot_nn(x3[s], nea[k])))
                terms.append((s, dot_nt(x3[f], nea[k])))
            for i in range(CPD):
                nacc[i] = add_where(nacc[i], terms, i)

        def gather_returned(gi):
            for copy in d_copies[gi]:
                copy.wait_recv()
            out = []
            for zi in groups[gi]:
                terms = []
                for dx in range(xd):
                    if zi == 0 and dx == 0:
                        continue
                    for j in range(MOST):
                        s = ((-dx) % xd) * per_x + zi * MOST + j
                        term = r_d[dx * per_x + zi * MOST + j].astype(F32)
                        terms.append((tabs[dx, 1, s], term))
                for i in range(CPD):
                    acc = add_where(jnp.zeros(terms[0][1].shape, F32), terms, i)
                    if zi == 0:
                        d_own[i] = acc
                    else:
                        zsend[zi, i] = acc.astype(BF16)
                if zi:
                    dz = dz_of[zi]
                    out.append(send(zsend.at[zi], zrecv.at[zi_of(-dz)], at(dz=dz)))
            return out

        def first_terms(gi):
            for copy in a_copies[gi]:
                copy.wait_recv()
            terms = []
            for zi in groups[gi]:
                for dx in range(xd):
                    if zi == 0 and dx == 0:
                        continue
                    for j in range(MOST):
                        s = dx * per_x + zi * MOST + j
                        terms.append((tabs[0, 2, s], dot_nn(r_a[s], cou[tabs[0, 3, s]])))
            for i in range(CPD):
                lacc[i] = add_where(lacc[i], terms, i)

        for i in range(CPD):
            lacc[i] = jnp.zeros_like(lacc[i])
        a_copies = {0: answer(0)}
        loads["sel"].wait()
        for i in range(CPD):
            nacc[i] = dot_nn(x3[i], sel[i])
        z_copies = gather_returned(len(groups) - 1)
        loads["nea"].wait()
        mid = near_count // 2
        for h in range(1, half + 1):
            for copy in hop:
                copy.wait_recv()
            if h < half:
                hop = ring(h + 1)
            a_copies[h] = answer(h)
            z_copies += gather_returned(len(groups) - 1 - h)
            if h == 1:
                near_pairs(0, mid)
            elif h == 2:
                near_pairs(mid, near_count)
            else:
                first_terms(h - 3)

        for copy in b_copies + c_copies:
            copy.wait_recv()
        v_terms = [
            (u_first[k], dot_nn(pbuf[u_dc[k], u_dy[k], u_row[k]], uco[k]))
            for k in range(upper_count)
        ]
        for p in range(P1D):
            acc = jnp.zeros(v_terms[0][1].shape, F32)
            for dy, dc in column:
                acc = acc + u_recv[dc, dy, p].astype(F32)
            pf[p] = add_where(acc, v_terms, p).astype(BF16)
        for gi in range(half - 2, half):
            first_terms(gi)
        for copy in z_copies:
            copy.wait_recv()
        for i in range(CPD):
            acc = lacc[i] + d_own[i] + dot_nt(pf[par_s[i] % P1D], tra[i])
            for zi in range(1, zd):
                acc = acc + zrecv[zi, i].astype(F32)
            lacc[i] = acc

        first_terms(half)
        for i in range(CPD):
            total = lacc[i].astype(BF16)
            out_ref[:, i * width:(i + 1) * width] = (nacc[i] + dot_nt(total, bas[i])).astype(BF16)
        for copy in sent:
            copy.wait_send()

    n_sems = (xd - 1) + 2 * half + 2 * len(column) + 2 * (xd - 1) * len(groups) + (zd - 1)
    return kernel, n_sems, xd * per_x


def solution(mesh):
    yd = mesh.shape["branch"] // CORES
    zd = mesh.shape["leaf"] // XDIM
    kernel, n_sems, nslots = make_kernel(yd, zd)

    def on_device(
        vectors, leaf_cluster_bases, transfers, parents, leaf_pairs, live_pairs, couplings,
        upper_pairs, upper_coupling_matrices, self_blocks, near_pairs, near_blocks,
    ):
        nv = vectors.shape[0]
        leaf, k = leaf_cluster_bases.shape[1:]
        any_ = pl.BlockSpec(memory_space=pl.ANY)
        smem = pl.BlockSpec(memory_space=pltpu.SMEM)
        vmem = pl.BlockSpec(memory_space=pltpu.VMEM)
        vm = pltpu.VMEM
        block = (nv, k)
        return pl.pallas_call(
            kernel,
            out_shape=jax.ShapeDtypeStruct(vectors.shape, BF16),
            in_specs=[any_, any_, any_, smem, vmem, smem, any_, smem, any_, any_, smem, any_],
            out_specs=vmem,
            scratch_shapes=[
                vm(vectors.shape, BF16), vm(leaf_cluster_bases.shape, BF16),
                vm(transfers.shape, BF16), vm(couplings.shape, BF16),
                vm(upper_coupling_matrices.shape, BF16), vm(self_blocks.shape, BF16),
                vm(near_blocks.shape, BF16),
                vm((XDIM, 8, LANES), jnp.int32), pltpu.SMEM((XDIM, 8, LANES), jnp.int32),
                vm((P1D,) + block, BF16),
                vm((nslots,) + block, BF16), vm((nslots,) + block, BF16),
                vm((nslots,) + block, BF16), vm((nslots,) + block, BF16),
                vm((couplings.shape[0] + 1,) + block, BF16),
                vm((zd, CPD) + block, BF16), vm((zd, CPD) + block, BF16),
                vm((CPD,) + block, F32),
                vm((CORES, yd, P1D) + block, BF16), vm((CORES, yd, P1D) + block, BF16),
                vm((CORES, yd, P1D) + block, BF16), vm((P1D,) + block, BF16),
                vm((CPD, nv, leaf), BF16), vm((CPD, nv, leaf), F32), vm((CPD,) + block, F32),
                pltpu.SemaphoreType.DMA((9,)),
                pltpu.SemaphoreType.DMA((n_sems,)), pltpu.SemaphoreType.DMA((n_sems,)),
            ] + [vm((CPD,) + block, BF16)] * zd,
            compiler_params=pltpu.CompilerParams(
                collective_id=0, has_side_effects=True, vmem_limit_bytes=56 * 1024 * 1024
            ),
            name="h2_apply",
        )(
            vectors, leaf_cluster_bases, transfers, parents, leaf_pairs.T, live_pairs, couplings,
            upper_pairs.T, upper_coupling_matrices, self_blocks, near_pairs.T, near_blocks,
        )

    both = ("branch", "leaf")
    return jax.shard_map(
        on_device,
        mesh=mesh,
        in_specs=(
            P(None, both), P(both, None, None), P(both, None, None), P(both), P(both, None),
            P(both), P(both, None, None), P(both, None), P(both, None, None),
            P(both, None, None), P(both, None), P(both, None, None),
        ),
        out_specs=P(None, both),
        check_vma=False,
    )
```

```python
import jax
import jax.numpy as jnp
from jax import lax
from jax.experimental import pallas as pl
from jax.experimental.pallas import tpu as pltpu
from jax.sharding import PartitionSpec as P

CPD = 6
P1D = 2
CORES = 2
XDIM = 4
MOST = 2
LANES = 128
FAR = 1000
MESH = pl.DeviceIdType.MESH
F32 = jnp.float32
BF16 = jnp.bfloat16
UNROLL = 8


def dot_nn(a, b):
    return jnp.dot(a, b, preferred_element_type=F32)


def dot_nt(a, b):
    return lax.dot_general(a, b, (((1,), (1,)), ((), ())), preferred_element_type=F32)


def make_kernel(yd, zd):
    cd, xd = CORES, XDIM
    per_x = zd * MOST
    half = zd // 2
    cut = CPD // 2
    assert zd == 8

    def zi_of(dz):
        dz %= zd
        if dz == 0:
            return 0
        return 2 * dz - 1 if dz <= half else 2 * (zd - dz)

    ask_groups = [[0], [1, 2, 3, 4], [5, 6, 7]]
    back_groups = [[0, 1, 2], [3, 4], [5, 6, 7]]
    column = [(dy, dc) for dc in range(cd) for dy in range(yd) if dy or dc]

    def kernel(
        vec_h, bas_h, tra_h, par_s, lp_v, live_v, cou_h, up_s, uco_h, sel_h, np_s, nea_h,
        out_ref,
        vec, bas, tra, cou, uco, sel, nea,
        tab, tabs, p_own, s_a, r_a, s_d, r_d, t_buf, zsend, zrecv, zin, d_own,
        up_send, up_recv, pf,
        x3, nacc, lacc,
        lsem, ssem, rsem, *zbuf,
    ):
        b = lax.axis_index("branch")
        l = lax.axis_index("leaf")
        y, c, z, x = b // cd, b % cd, l // xd, l % xd
        pair_count = cou_h.shape[0]
        upper_count = uco_h.shape[0]
        near_count = nea_h.shape[0]
        width = x3.shape[2]

        def at(dy=0, dc=0, dz=0, dx=0):
            yy, cc = (y + dy) % yd, (c + dc) % cd
            zz, xx = (z + dz) % zd, (x + dx) % xd
            return (yy * cd + cc, zz * xd + xx)

        loads = {}
        for i, (name, src, dst) in enumerate(
            (("vec", vec_h, vec), ("bas", bas_h, bas), ("tra", tra_h, tra), ("cou", cou_h, cou),
             ("uco", uco_h, uco), ("sel", sel_h, sel), ("nea", nea_h, nea))
        ):
            loads[name] = pltpu.make_async_copy(src, dst, lsem.at[i])
            loads[name].start()

        barrier = pltpu.get_barrier_semaphore()
        partners = [at(dz=d) for d in range(1, zd)] + [at(dx=d) for d in range(1, xd)]
        partners += [at(dy=dy, dc=dc) for dy, dc in column]
        for device in partners:
            pl.semaphore_signal(barrier, inc=1, device_id=device, device_id_type=MESH)

        count = [0]
        sent = []

        def send(src, dst, device):
            i = count[0]
            count[0] += 1
            copy = pltpu.make_async_remote_copy(
                src_ref=src, dst_ref=dst, send_sem=ssem.at[i], recv_sem=rsem.at[i],
                device_id=device, device_id_type=MESH,
            )
            copy.start()
            sent.append(copy)
            return copy

        def add_where(acc, terms, i):
            for where, term in terms:
                acc = acc + jnp.where(where == i, term, 0.0)
            return acc

        live = live_v[...]
        first = lp_v[0:1, :] % CPD
        second = lp_v[1:2, :] % (zd * xd * CPD)
        owner = (second * 10923) >> 16
        second_c = second - owner * CPD
        oz, ox = owner // xd, owner % xd
        odz = (oz - z + zd) % zd
        odx = (ox - x + xd) % xd
        ozi = jnp.where(odz <= half, 2 * odz - 1, 2 * (zd - odz))
        ozi = jnp.where(odz == 0, 0, ozi)
        peer = odx * zd + ozi
        sub = lax.broadcasted_iota(jnp.int32, (pair_count, pair_count), 0)
        lane = lax.broadcasted_iota(jnp.int32, (pair_count, pair_count), 1)
        eye = sub == lane

        def to_col(row):
            return jnp.sum(jnp.where(eye, row, 0), axis=1, keepdims=True)

        peer_col = to_col(peer)
        rank_col = jnp.sum(
            jnp.where((peer == peer_col) & (lane < sub), 1, 0), axis=1, keepdims=True
        )
        sub_col = lax.broadcasted_iota(jnp.int32, (pair_count, 1), 0)
        pos_col = jnp.where(sub_col < live, peer_col * MOST + rank_col, FAR)
        slot_lane = lax.broadcasted_iota(jnp.int32, (pair_count, LANES), 1)
        hit = pos_col == slot_lane

        def by_slot(col, none):
            return none - jnp.sum(jnp.where(hit, none - col, 0), axis=0, keepdims=True)

        pair_of = by_slot(sub_col, pair_count)
        tab[0] = jnp.zeros_like(tab[0])
        tab[0, 0:1, :] = pair_of
        tab[0, 1:2, :] = by_slot(to_col(second_c), 0)
        tab[0, 2:3, :] = by_slot(to_col(first), CPD)
        tab[0, 3:4, :] = jnp.minimum(pair_of, pair_count - 1)
        tab[0, 4:5, 0:pair_count] = first
        own_tab = pltpu.make_async_copy(tab.at[0], tabs.at[0], lsem.at[7])
        own_tab.start()

        loads["vec"].wait()
        loads["bas"].wait()
        for i in range(CPD):
            xi = vec[:, i * width:(i + 1) * width]
            x3[i] = xi
            zbuf[0][i] = dot_nn(xi, bas[i]).astype(BF16)

        loads["tra"].wait()
        lifted = [(par_s[i] % P1D, dot_nn(zbuf[0][i], tra[i])) for i in range(CPD)]
        for p in range(P1D):
            acc = add_where(jnp.zeros(lifted[0][1].shape, F32), lifted, p).astype(BF16)
            p_own[p] = acc
            for dy, dc in column:
                up_send[dc, dy, p] = acc

        loads["cou"].wait()
        own_tab.wait()
        t_buf[pair_count] = jnp.zeros_like(t_buf[pair_count])

        def second_body(i, carry):
            for u in range(UNROLL):
                k = i * UNROLL + u
                f = tabs[0, 4, k]
                t_buf[k] = dot_nt(zbuf[0][f], cou[k]).astype(BF16)
            return carry

        lax.fori_loop(0, pair_count // UNROLL, second_body, 0)
        for dx in range(xd):
            buf = r_d if dx == 0 else s_d
            for s in range(dx * per_x, (dx + 1) * per_x):
                buf[s] = t_buf[tabs[0, 0, s]]

        loads["uco"].wait()
        u_first = [up_s[0, k] % P1D for k in range(upper_count)]
        u_row, u_dy, u_dc = [], [], []
        for k in range(upper_count):
            q = up_s[1, k]
            far_b = q // (P1D * zd * xd)
            u_row.append(q % P1D)
            u_dy.append((far_b // cd - y + yd) % yd)
            u_dc.append((far_b % cd - c + cd) % cd)
        u_terms = [
            ((u_dc[k] * yd + u_dy[k]) * P1D + u_row[k], dot_nt(p_own[u_first[k]], uco[k]))
            for k in range(upper_count)
        ]
        for dy, dc in column:
            for p in range(P1D):
                acc = jnp.zeros(u_terms[0][1].shape, F32)
                up_send[dc, dy, P1D + p] = add_where(acc, u_terms, (dc * yd + dy) * P1D + p).astype(BF16)

        pl.semaphore_wait(barrier, len(partners))

        def send_slots(src, dst, group):
            lo, n = group[0] * MOST, len(group) * MOST
            return [
                send(
                    src.at[pl.ds(dx * per_x + lo, n)],
                    dst.at[pl.ds(((-dx) % xd) * per_x + lo, n)],
                    at(dx=dx),
                )
                for dx in range(1, xd)
            ]

        near_z = {d: send(zbuf[0], zbuf[zi_of(-d)], at(dz=d)) for d in (2, -2, 1, -1)}
        tab_copies = [send(tab.at[0], tab.at[(-d) % xd], at(dx=d)) for d in range(1, xd)]
        back_copies = {gi: send_slots(s_d, r_d, back_groups[gi]) for gi in (2, 1, 0)}
        up_copies = [
            send(up_send.at[dc, dy], up_recv.at[(-dc) % cd, (-dy) % yd], at(dy=dy, dc=dc))
            for dy, dc in column
        ]

        for i in range(CPD):
            lacc[i] = jnp.zeros_like(lacc[i])
        loads["sel"].wait()
        for i in range(CPD):
            nacc[i] = dot_nn(x3[i], sel[i])

        for copy in tab_copies:
            copy.wait_recv()
        peer_tab = pltpu.make_async_copy(tab.at[1:xd], tabs.at[1:xd], lsem.at[8])
        peer_tab.start()
        peer_tab.wait()

        def answer(gi):
            for dx in range(xd):
                for zi in ask_groups[gi]:
                    for j in range(MOST):
                        r = tabs[dx, 1, ((-dx) % xd) * per_x + zi * MOST + j]
                        buf = r_a if dx == 0 else s_a
                        buf[dx * per_x + zi * MOST + j] = zbuf[zi][r]
            return send_slots(s_a, r_a, ask_groups[gi])

        def near_pairs(lo, hi):
            terms = []
            for k in range(lo, hi):
                f, s = np_s[0, k] % CPD, np_s[1, k] % CPD
                terms.append((f, dot_nn(x3[s], nea[k])))
                terms.append((s, dot_nt(x3[f], nea[k])))
            for i in range(CPD):
                nacc[i] = add_where(nacc[i], terms, i)

        def returned(zi):
            terms = []
            for dx in range(xd):
                if zi == 0 and dx == 0:
                    continue
                for j in range(MOST):
                    s = ((-dx) % xd) * per_x + zi * MOST + j
                    term = r_d[dx * per_x + zi * MOST + j].astype(F32)
                    terms.append((tabs[dx, 1, s], term))
            return [add_where(jnp.zeros(terms[0][1].shape, F32), terms, i) for i in range(CPD)]

        def first_terms(gi):
            for copy in ask_copies[gi]:
                copy.wait_recv()
            terms = []
            for zi in ask_groups[gi]:
                for dx in range(xd):
                    if zi == 0 and dx == 0:
                        continue
                    for j in range(MOST):
                        s = dx * per_x + zi * MOST + j
                        terms.append((tabs[0, 2, s], dot_nn(r_a[s], cou[tabs[0, 3, s]])))
            for i in range(CPD):
                lacc[i] = add_where(lacc[i], terms, i)

        ask_copies = [answer(0)]

        far_z = []
        for d in (2, -2):
            near_z[-d].wait_recv()
            unit = d // 2
            block = zbuf[zi_of(d)]
            lo, hi = (0, cut) if d > 0 else (cut, CPD)
            far_z.append(send(block, zbuf[zi_of(d + unit)], at(dz=-unit)))
            far_z.append(send(block.at[lo:hi], zbuf[zi_of(2 * d)].at[lo:hi], at(dz=-d)))

        for copy in back_copies[2]:
            copy.wait_recv()
        mid_z = {}
        for d in (3, -3, 4):
            for i, acc in enumerate(returned(zi_of(d))):
                zsend[zi_of(d), i] = acc.astype(BF16)
            if d != 4:
                unit = 1 if d > 0 else -1
                mid_z[d] = [send(zsend.at[zi_of(d)], zin.at[zi_of(d)], at(dz=unit))]
        for unit, lo, hi in ((1, cut, CPD), (-1, 0, cut)):
            mid_z[3 * unit].append(
                send(zsend.at[zi_of(4), lo:hi], zin.at[zi_of(4), lo:hi], at(dz=2 * unit))
            )

        for d in (1, -1):
            near_z[-d].wait_recv()
        ask_copies.append(answer(1))

        loads["nea"].wait()
        near_pairs(0, near_count // 2)

        for copy in back_copies[1]:
            copy.wait_recv()
        last_z = []
        for unit, lo, hi in ((1, cut, CPD), (-1, 0, cut)):
            for copy in mid_z[3 * unit]:
                copy.wait_recv()
            zi = zi_of(2 * unit)
            for i, acc in enumerate(returned(zi)):
                acc = acc + zin[zi_of(3 * unit), i].astype(F32)
                if lo <= i < hi:
                    acc = acc + zin[zi_of(4), i].astype(F32)
                zsend[zi, i] = acc.astype(BF16)
            last_z.append(send(zsend.at[zi], zrecv.at[zi_of(-2 * unit)], at(dz=2 * unit)))
        for copy in back_copies[0]:
            copy.wait_recv()
        for d in (1, -1):
            zi = zi_of(d)
            for i, acc in enumerate(returned(zi)):
                zsend[zi, i] = acc.astype(BF16)
            last_z.append(send(zsend.at[zi], zrecv.at[zi_of(-d)], at(dz=d)))
        for i, acc in enumerate(returned(0)):
            d_own[i] = acc

        for copy in far_z:
            copy.wait_recv()
        ask_copies.append(answer(2))
        near_pairs(near_count // 2, near_count)
        first_terms(0)
        first_terms(1)

        for copy in up_copies:
            copy.wait_recv()
        v_terms = [
            (u_first[k], dot_nn(up_recv[u_dc[k], u_dy[k], u_row[k]], uco[k]))
            for k in range(upper_count)
        ]
        for p in range(P1D):
            acc = jnp.zeros(v_terms[0][1].shape, F32)
            for dy, dc in column:
                acc = acc + up_recv[dc, dy, P1D + p].astype(F32)
            pf[p] = add_where(acc, v_terms, p).astype(BF16)
        lowered = [dot_nt(pf[par_s[i] % P1D], tra[i]) for i in range(CPD)]
        for copy in last_z:
            copy.wait_recv()
        for i in range(CPD):
            acc = lacc[i] + d_own[i] + lowered[i]
            for zi in range(1, 5):
                acc = acc + zrecv[zi, i].astype(F32)
            lacc[i] = acc

        first_terms(2)
        for i in range(CPD):
            total = lacc[i].astype(BF16)
            out_ref[:, i * width:(i + 1) * width] = (nacc[i] + dot_nt(total, bas[i])).astype(BF16)
        for copy in sent:
            copy.wait_send()

    n_sems = 8 + 8 + len(column) + (xd - 1) * (1 + len(ask_groups) + len(back_groups))
    return kernel, n_sems, xd * per_x


def solution(mesh):
    yd = mesh.shape["branch"] // CORES
    zd = mesh.shape["leaf"] // XDIM
    kernel, n_sems, nslots = make_kernel(yd, zd)

    def on_device(
        vectors, leaf_cluster_bases, transfers, parents, leaf_pairs, live_pairs, couplings,
        upper_pairs, upper_coupling_matrices, self_blocks, near_pairs, near_blocks,
    ):
        nv = vectors.shape[0]
        leaf, k = leaf_cluster_bases.shape[1:]
        any_ = pl.BlockSpec(memory_space=pl.ANY)
        smem = pl.BlockSpec(memory_space=pltpu.SMEM)
        vmem = pl.BlockSpec(memory_space=pltpu.VMEM)
        vm = pltpu.VMEM
        block = (nv, k)
        return pl.pallas_call(
            kernel,
            out_shape=pltpu.VMEM(vectors.shape, BF16),
            in_specs=[any_, any_, any_, smem, vmem, vmem, any_, smem, any_, any_, smem, any_],
            out_specs=vmem,
            scratch_shapes=[
                vm(vectors.shape, BF16), vm(leaf_cluster_bases.shape, BF16),
                vm(transfers.shape, BF16), vm(couplings.shape, BF16),
                vm(upper_coupling_matrices.shape, BF16), vm(self_blocks.shape, BF16),
                vm(near_blocks.shape, BF16),
                vm((XDIM, 8, LANES), jnp.int32), pltpu.SMEM((XDIM, 8, LANES), jnp.int32),
                vm((P1D,) + block, BF16),
                vm((nslots,) + block, BF16), vm((nslots,) + block, BF16),
                vm((nslots,) + block, BF16), vm((nslots,) + block, BF16),
                vm((couplings.shape[0] + 1,) + block, BF16),
                vm((zd, CPD) + block, BF16), vm((zd, CPD) + block, BF16),
                vm((zd, CPD) + block, BF16), vm((CPD,) + block, F32),
                vm((CORES, yd, 2 * P1D) + block, BF16), vm((CORES, yd, 2 * P1D) + block, BF16),
                vm((P1D,) + block, BF16),
                vm((CPD, nv, leaf), BF16), vm((CPD, nv, leaf), F32), vm((CPD,) + block, F32),
                pltpu.SemaphoreType.DMA((9,)),
                pltpu.SemaphoreType.DMA((n_sems,)), pltpu.SemaphoreType.DMA((n_sems,)),
            ] + [vm((CPD,) + block, BF16)] * zd,
            compiler_params=pltpu.CompilerParams(
                collective_id=0, has_side_effects=True, vmem_limit_bytes=56 * 1024 * 1024
            ),
            name="h2_apply",
        )(
            vectors, leaf_cluster_bases, transfers, parents, leaf_pairs.T, live_pairs.reshape(1, 1), couplings,
            upper_pairs.T, upper_coupling_matrices, self_blocks, near_pairs.T, near_blocks,
        )

    both = ("branch", "leaf")
    return jax.shard_map(
        on_device,
        mesh=mesh,
        in_specs=(
            P(None, both), P(both, None, None), P(both, None, None), P(both), P(both, None),
            P(both), P(both, None, None), P(both, None), P(both, None, None),
            P(both, None, None), P(both, None), P(both, None, None),
        ),
        out_specs=P(None, both),
        check_vma=False,
    )
```

```python
import functools

import jax
import jax.numpy as jnp
from jax import lax
from jax.experimental import pallas as pl
from jax.experimental.pallas import tpu as pltpu
from jax.sharding import PartitionSpec as P

CPD = 6
P1D = 2
CORES = 2
XDIM = 4
MOST = 2
LANES = 128
FAR = 1000
MESH = pl.DeviceIdType.MESH
F32 = jnp.float32
BF16 = jnp.bfloat16
UNROLL = 8


def dot_nn(a, b):
    return jnp.dot(a, b, preferred_element_type=F32)


def dot_nt(a, b):
    return lax.dot_general(a, b, (((1,), (1,)), ((), ())), preferred_element_type=F32)


def make_kernel(yd, zd):
    cd, xd = CORES, XDIM
    per_x = zd * MOST
    half = zd // 2
    cut = CPD // 2
    assert zd == 8

    def zi_of(dz):
        dz %= zd
        if dz == 0:
            return 0
        return 2 * dz - 1 if dz <= half else 2 * (zd - dz)

    ask_groups = [[0], [1, 2, 3, 4], [5, 6, 7]]
    back_groups = [[0, 1, 2], [3, 4], [5, 6, 7]]
    column = [(dy, 0) for dy in range(1, yd)] + [(0, 1)]

    def kernel(
        vec_h, bas_h, tra_h, par_s, lp_v, live_v, cou_h, up_s, uco_h, sel_h, np_s, nea_h,
        out_ref,
        vec, bas, tra, cou, uco, sel, nea,
        tab, tabs, p_own, s_a, r_a, s_d, r_d, t_buf, zsend, zrecv, zin, d_own,
        pbuf, u_send, u_recv, u_acc, c_send, c_recv, pf,
        x3, nacc, lacc,
        lsem, ssem, rsem, row_ok, col_ok, *zbuf,
    ):
        b = lax.axis_index("branch")
        l = lax.axis_index("leaf")
        y, c, z, x = b // cd, b % cd, l // xd, l % xd
        pair_count = cou_h.shape[0]
        upper_count = uco_h.shape[0]
        near_count = nea_h.shape[0]
        width = x3.shape[2]

        def at(dy=0, dc=0, dz=0, dx=0):
            yy, cc = (y + dy) % yd, (c + dc) % cd
            zz, xx = (z + dz) % zd, (x + dx) % xd
            return (yy * cd + cc, zz * xd + xx)

        barrier = pltpu.get_barrier_semaphore()
        row = [(at(dz=d), (z + d) % zd > z) for d in (1, -1, 2, -2)]
        row += [(at(dx=d), (x + d) % xd > x) for d in range(1, xd)]

        def turn(yy):
            return jnp.where(yy < yd // 2, yy, yd + yd // 2 - 1 - yy)

        col = [
            (at(dy=dy, dc=dc), turn((y + dy) % yd) > turn(y) if dy else c == 0)
            for dy, dc in column
        ]

        def signal(sem, device):
            pl.semaphore_signal(sem, inc=1, device_id=device, device_id_type=MESH)

        def wait_some(sem, amount):
            pl.when(amount > 0)(lambda: pl.semaphore_wait(sem, amount))

        def number(partners, want_later):
            flags = [later if want_later else jnp.logical_not(later) for _, later in partners]
            return sum(jnp.where(flag, 1, 0) for flag in flags)

        for device, later in row + col:
            pl.when(later)(functools.partial(signal, barrier, device))

        loads = {}
        for i, (name, src, dst) in enumerate(
            (("vec", vec_h, vec), ("bas", bas_h, bas), ("tra", tra_h, tra), ("cou", cou_h, cou),
             ("uco", uco_h, uco), ("sel", sel_h, sel), ("nea", nea_h, nea))
        ):
            loads[name] = pltpu.make_async_copy(src, dst, lsem.at[i])
            loads[name].start()

        count = [0]
        sent = []

        def ready(src, dst, device):
            i = count[0]
            count[0] += 1
            copy = pltpu.make_async_remote_copy(
                src_ref=src, dst_ref=dst, send_sem=ssem.at[i], recv_sem=rsem.at[i],
                device_id=device, device_id_type=MESH,
            )
            sent.append(copy)
            return copy

        def send(src, dst, device):
            copy = ready(src, dst, device)
            copy.start()
            return copy

        def add_where(acc, terms, i):
            for where, term in terms:
                acc = acc + jnp.where(where == i, term, 0.0)
            return acc

        wait_some(barrier, number(row + col, False))
        for sem, partners in ((row_ok, row), (col_ok, col)):
            for device, later in partners:
                pl.when(jnp.logical_not(later))(functools.partial(signal, sem, device))

        live = live_v[...]
        first = lp_v[0:1, :] % CPD
        second = lp_v[1:2, :] % (zd * xd * CPD)
        owner = (second * 10923) >> 16
        second_c = second - owner * CPD
        oz, ox = owner // xd, owner % xd
        odz = (oz - z + zd) % zd
        odx = (ox - x + xd) % xd
        ozi = jnp.where(odz <= half, 2 * odz - 1, 2 * (zd - odz))
        ozi = jnp.where(odz == 0, 0, ozi)
        peer = odx * zd + ozi
        sub = lax.broadcasted_iota(jnp.int32, (pair_count, pair_count), 0)
        lane = lax.broadcasted_iota(jnp.int32, (pair_count, pair_count), 1)
        eye = sub == lane

        def to_col(row):
            return jnp.sum(jnp.where(eye, row, 0), axis=1, keepdims=True)

        peer_col = to_col(peer)
        rank_col = jnp.sum(
            jnp.where((peer == peer_col) & (lane < sub), 1, 0), axis=1, keepdims=True
        )
        sub_col = lax.broadcasted_iota(jnp.int32, (pair_count, 1), 0)
        pos_col = jnp.where(sub_col < live, peer_col * MOST + rank_col, FAR)
        slot_lane = lax.broadcasted_iota(jnp.int32, (pair_count, LANES), 1)
        hit = pos_col == slot_lane

        def by_slot(col, none):
            return none - jnp.sum(jnp.where(hit, none - col, 0), axis=0, keepdims=True)

        pair_of = by_slot(sub_col, pair_count)
        tab[0] = jnp.zeros_like(tab[0])
        tab[0, 0:1, :] = pair_of
        tab[0, 1:2, :] = by_slot(to_col(second_c), 0)
        tab[0, 2:3, :] = by_slot(to_col(first), CPD)
        tab[0, 3:4, :] = jnp.minimum(pair_of, pair_count - 1)
        tab[0, 4:5, 0:pair_count] = first
        own_tab = pltpu.make_async_copy(tab.at[0], tabs.at[0], lsem.at[7])
        own_tab.start()

        loads["vec"].wait()
        loads["bas"].wait()
        for i in range(CPD):
            xi = vec[:, i * width:(i + 1) * width]
            x3[i] = xi
            zbuf[0][i] = dot_nn(xi, bas[i]).astype(BF16)

        def send_slots(src, dst, group, begin=ready):
            lo, n = group[0] * MOST, len(group) * MOST
            return [
                begin(
                    src.at[pl.ds(dx * per_x + lo, n)],
                    dst.at[pl.ds(((-dx) % xd) * per_x + lo, n)],
                    at(dx=dx),
                )
                for dx in range(1, xd)
            ]

        near_z = {d: ready(zbuf[0], zbuf[zi_of(-d)], at(dz=d)) for d in (2, -2, 1, -1)}
        tab_copies = [ready(tab.at[0], tab.at[(-d) % xd], at(dx=d)) for d in range(1, xd)]

        def start_row():
            wait_some(row_ok, number(row, True))
            for copy in tab_copies + list(near_z.values()):
                copy.start()

        pl.when(z >= half)(start_row)

        loads["cou"].wait()
        own_tab.wait()
        t_buf[pair_count] = jnp.zeros_like(t_buf[pair_count])

        def second_body(i, carry):
            for u in range(UNROLL):
                k = i * UNROLL + u
                f = tabs[0, 4, k]
                t_buf[k] = dot_nt(zbuf[0][f], cou[k]).astype(BF16)
            return carry

        lax.fori_loop(0, pair_count // UNROLL, second_body, 0)
        for dx in range(xd):
            buf = r_d if dx == 0 else s_d
            for s in range(dx * per_x, (dx + 1) * per_x):
                buf[s] = t_buf[tabs[0, 0, s]]

        back_copies = {gi: send_slots(s_d, r_d, back_groups[gi]) for gi in (2, 1, 0)}

        def start_back():
            for gi in (2, 1, 0):
                for copy in back_copies[gi]:
                    copy.start()

        pl.when(z >= half)(start_back)

        loads["tra"].wait()
        lifted = [(par_s[i] % P1D, dot_nn(zbuf[0][i], tra[i])) for i in range(CPD)]
        for p in range(P1D):
            acc = add_where(jnp.zeros(lifted[0][1].shape, F32), lifted, p).astype(BF16)
            p_own[p] = acc
            pbuf[0, 0, p] = acc

        loads["uco"].wait()
        u_first = [up_s[0, k] % P1D for k in range(upper_count)]
        u_row, u_dy, u_dc = [], [], []
        for k in range(upper_count):
            q = up_s[1, k]
            far_b = q // (P1D * zd * xd)
            u_row.append(q % P1D)
            u_dy.append((far_b // cd - y + yd) % yd)
            u_dc.append((far_b % cd - c + cd) % cd)
        u_terms = [
            ((u_dc[k] * yd + u_dy[k]) * P1D + u_row[k], dot_nt(p_own[u_first[k]], uco[k]))
            for k in range(upper_count)
        ]
        for dy in range(yd):
            for p in range(P1D):
                acc = jnp.zeros(u_terms[0][1].shape, F32)
                u_send[dy, p] = add_where(acc, u_terms, (yd + dy) * P1D + p).astype(BF16)
                u_acc[dy, p] = add_where(acc, u_terms, dy * P1D + p)
        part_copy = ready(u_send, u_recv, at(dc=1))
        own_copy = ready(p_own, pbuf.at[1, 0], at(dc=1))
        up_copies = [
            ready(p_own, pbuf.at[0, (-dy) % yd], at(dy=dy)) for dy in range(1, yd)
        ]

        def start_upper():
            wait_some(col_ok, number(col, True))
            for copy in [part_copy, own_copy] + up_copies:
                copy.start()

        start_upper()

        @pl.when(z < half)
        def _():
            start_row()
            start_back()


        far_z = []
        for d in (2, -2):
            near_z[-d].wait_recv()
            unit = d // 2
            block = zbuf[zi_of(d)]
            lo, hi = (0, cut) if d > 0 else (cut, CPD)
            far_z.append(send(block, zbuf[zi_of(d + unit)], at(dz=-unit)))
            far_z.append(send(block.at[lo:hi], zbuf[zi_of(2 * d)].at[lo:hi], at(dz=-d)))

        for i in range(CPD):
            lacc[i] = jnp.zeros_like(lacc[i])
        loads["sel"].wait()
        for i in range(CPD):
            nacc[i] = dot_nn(x3[i], sel[i])

        for copy in tab_copies:
            copy.wait_recv()
        peer_tab = pltpu.make_async_copy(tab.at[1:xd], tabs.at[1:xd], lsem.at[8])
        peer_tab.start()
        peer_tab.wait()

        def answer(gi):
            for dx in range(xd):
                for zi in ask_groups[gi]:
                    for j in range(MOST):
                        r = tabs[dx, 1, ((-dx) % xd) * per_x + zi * MOST + j]
                        buf = r_a if dx == 0 else s_a
                        buf[dx * per_x + zi * MOST + j] = zbuf[zi][r]
            return send_slots(s_a, r_a, ask_groups[gi], send)

        def near_pairs(lo, hi):
            terms = []
            for k in range(lo, hi):
                f, s = np_s[0, k] % CPD, np_s[1, k] % CPD
                terms.append((f, dot_nn(x3[s], nea[k])))
                terms.append((s, dot_nt(x3[f], nea[k])))
            for i in range(CPD):
                nacc[i] = add_where(nacc[i], terms, i)

        def returned(zi):
            terms = []
            for dx in range(xd):
                if zi == 0 and dx == 0:
                    continue
                for j in range(MOST):
                    s = ((-dx) % xd) * per_x + zi * MOST + j
                    term = r_d[dx * per_x + zi * MOST + j].astype(F32)
                    terms.append((tabs[dx, 1, s], term))
            return [add_where(jnp.zeros(terms[0][1].shape, F32), terms, i) for i in range(CPD)]

        def first_terms(gi):
            for copy in ask_copies[gi]:
                copy.wait_recv()
            terms = []
            for zi in ask_groups[gi]:
                for dx in range(xd):
                    if zi == 0 and dx == 0:
                        continue
                    for j in range(MOST):
                        s = dx * per_x + zi * MOST + j
                        terms.append((tabs[0, 2, s], dot_nn(r_a[s], cou[tabs[0, 3, s]])))
            for i in range(CPD):
                lacc[i] = add_where(lacc[i], terms, i)

        ask_copies = [answer(0)]

        for copy in back_copies[2]:
            copy.wait_recv()
        mid_z = {}
        for d in (3, -3, 4):
            for i, acc in enumerate(returned(zi_of(d))):
                zsend[zi_of(d), i] = acc.astype(BF16)
            if d != 4:
                unit = 1 if d > 0 else -1
                mid_z[d] = [send(zsend.at[zi_of(d)], zin.at[zi_of(d)], at(dz=unit))]
        for unit, lo, hi in ((1, cut, CPD), (-1, 0, cut)):
            mid_z[3 * unit].append(
                send(zsend.at[zi_of(4), lo:hi], zin.at[zi_of(4), lo:hi], at(dz=2 * unit))
            )

        for d in (1, -1):
            near_z[-d].wait_recv()
        ask_copies.append(answer(1))

        part_copy.wait_recv()
        for dy in range(yd):
            for p in range(P1D):
                acc = u_acc[dy, p] + u_recv[dy, p].astype(F32)
                if dy:
                    c_send[dy, p] = acc.astype(BF16)
                else:
                    u_acc[dy, p] = acc
        sum_copies = [
            send(c_send.at[dy], c_recv.at[(-dy) % yd], at(dy=dy)) for dy in range(1, yd)
        ]

        for copy in far_z:
            copy.wait_recv()
        ask_copies.append(answer(2))

        for copy in back_copies[1]:
            copy.wait_recv()
        last_z = []
        for unit, lo, hi in ((1, cut, CPD), (-1, 0, cut)):
            for copy in mid_z[3 * unit]:
                copy.wait_recv()
            zi = zi_of(2 * unit)
            for i, acc in enumerate(returned(zi)):
                acc = acc + zin[zi_of(3 * unit), i].astype(F32)
                if lo <= i < hi:
                    acc = acc + zin[zi_of(4), i].astype(F32)
                zsend[zi, i] = acc.astype(BF16)
            last_z.append(send(zsend.at[zi], zrecv.at[zi_of(-2 * unit)], at(dz=2 * unit)))
        for copy in back_copies[0]:
            copy.wait_recv()
        for d in (1, -1):
            zi = zi_of(d)
            for i, acc in enumerate(returned(zi)):
                zsend[zi, i] = acc.astype(BF16)
            last_z.append(send(zsend.at[zi], zrecv.at[zi_of(-d)], at(dz=d)))
        for i, acc in enumerate(returned(0)):
            d_own[i] = acc

        loads["nea"].wait()
        near_pairs(0, near_count // 2)
        for copy in up_copies:
            copy.wait_recv()
        share_copy = send(pbuf.at[0, 1:yd], pbuf.at[1, 1:yd], at(dc=1))
        near_pairs(near_count // 2, near_count)
        first_terms(0)
        first_terms(1)

        for copy in [own_copy, share_copy] + sum_copies:
            copy.wait_recv()
        v_terms = [
            (u_first[k], dot_nn(pbuf[u_dc[k], u_dy[k], u_row[k]], uco[k]))
            for k in range(upper_count)
        ]
        for p in range(P1D):
            acc = u_acc[0, p]
            for dy in range(1, yd):
                acc = acc + c_recv[dy, p].astype(F32)
            pf[p] = add_where(acc, v_terms, p).astype(BF16)
        lowered = [dot_nt(pf[par_s[i] % P1D], tra[i]) for i in range(CPD)]
        first_terms(2)
        for copy in last_z:
            copy.wait_recv()
        for i in range(CPD):
            acc = lacc[i] + d_own[i] + lowered[i]
            for zi in range(1, 5):
                acc = acc + zrecv[zi, i].astype(F32)
            total = acc.astype(BF16)
            out_ref[:, i * width:(i + 1) * width] = (nacc[i] + dot_nt(total, bas[i])).astype(BF16)
        for copy in sent:
            copy.wait_send()

    n_sems = 8 + 8 + 2 * yd + 1 + (xd - 1) * (1 + len(ask_groups) + len(back_groups))
    return kernel, n_sems, xd * per_x


def solution(mesh):
    yd = mesh.shape["branch"] // CORES
    zd = mesh.shape["leaf"] // XDIM
    kernel, n_sems, nslots = make_kernel(yd, zd)

    def on_device(
        vectors, leaf_cluster_bases, transfers, parents, leaf_pairs, live_pairs, couplings,
        upper_pairs, upper_coupling_matrices, self_blocks, near_pairs, near_blocks,
    ):
        nv = vectors.shape[0]
        leaf, k = leaf_cluster_bases.shape[1:]
        any_ = pl.BlockSpec(memory_space=pl.ANY)
        smem = pl.BlockSpec(memory_space=pltpu.SMEM)
        vmem = pl.BlockSpec(memory_space=pltpu.VMEM)
        vm = pltpu.VMEM
        block = (nv, k)
        return pl.pallas_call(
            kernel,
            out_shape=pltpu.VMEM(vectors.shape, BF16),
            in_specs=[any_, any_, any_, smem, vmem, vmem, any_, smem, any_, any_, smem, any_],
            out_specs=vmem,
            scratch_shapes=[
                vm(vectors.shape, BF16), vm(leaf_cluster_bases.shape, BF16),
                vm(transfers.shape, BF16), vm(couplings.shape, BF16),
                vm(upper_coupling_matrices.shape, BF16), vm(self_blocks.shape, BF16),
                vm(near_blocks.shape, BF16),
                vm((XDIM, 8, LANES), jnp.int32), pltpu.SMEM((XDIM, 8, LANES), jnp.int32),
                vm((P1D,) + block, BF16),
                vm((nslots,) + block, BF16), vm((nslots,) + block, BF16),
                vm((nslots,) + block, BF16), vm((nslots,) + block, BF16),
                vm((couplings.shape[0] + 1,) + block, BF16),
                vm((zd, CPD) + block, BF16), vm((zd, CPD) + block, BF16),
                vm((zd, CPD) + block, BF16), vm((CPD,) + block, F32),
                vm((CORES, yd, P1D) + block, BF16),
                vm((yd, P1D) + block, BF16), vm((yd, P1D) + block, BF16),
                vm((yd, P1D) + block, F32),
                vm((yd, P1D) + block, BF16), vm((yd, P1D) + block, BF16),
                vm((P1D,) + block, BF16),
                vm((CPD, nv, leaf), BF16), vm((CPD, nv, leaf), F32), vm((CPD,) + block, F32),
                pltpu.SemaphoreType.DMA((9,)),
                pltpu.SemaphoreType.DMA((n_sems,)), pltpu.SemaphoreType.DMA((n_sems,)),
                pltpu.SemaphoreType.REGULAR, pltpu.SemaphoreType.REGULAR,
            ] + [vm((CPD,) + block, BF16)] * zd,
            compiler_params=pltpu.CompilerParams(
                collective_id=0, has_side_effects=True, vmem_limit_bytes=56 * 1024 * 1024
            ),
            name="h2_apply",
        )(
            vectors, leaf_cluster_bases, transfers, parents, leaf_pairs.T, live_pairs.reshape(1, 1), couplings,
            upper_pairs.T, upper_coupling_matrices, self_blocks, near_pairs.T, near_blocks,
        )

    both = ("branch", "leaf")
    return jax.shard_map(
        on_device,
        mesh=mesh,
        in_specs=(
            P(None, both), P(both, None, None), P(both, None, None), P(both), P(both, None),
            P(both), P(both, None, None), P(both, None), P(both, None, None),
            P(both, None, None), P(both, None), P(both, None, None),
        ),
        out_specs=P(None, both),
        check_vma=False,
    )
```
